32 devices in a mesh: sx: 4 (over z), sy: 4 (over y, core), ev: 2 (over x).
Axes of the slice: x: 2, y: 2, z: 4, core: 2. Of those that a mesh axis runs over, the one named last changes fastest.
Arguments:
- adjoint_state: float32 [2, 9, 32, 32, 128], P('ev', None, 'sx', 'sy'), may hold values from -6 to 6
- forward_state: bfloat16 [2, 3, 9, 32, 32, 128], P('ev', None, None, 'sx', 'sy'), may hold values from -6 to 6
- inv_density: float32 [32, 32, 128], P('sx', 'sy'), may hold values from 0.6 to 1.6
- lame_lambda: float32 [32, 32, 128], P('sx', 'sy'), may hold values from 0.15 to 0.5
- shear_modulus: float32 [32, 32, 128], P('sx', 'sy'), may hold values from 0.1 to 0.4
- station_block: int32 [2, 512, 1], P('ev', ('sx', 'sy')), may hold values from 0 to 3; in each aligned block of 32 rows (0 to 31, 32 to 63, ..., all dimensions but the last counted through in order) at most 16 rows name the same one
- station_cell: int32 [2, 512], P('ev', ('sx', 'sy')), may hold values from 0 to 63
- station_trace: float32 [2, 512, 9], P('ev', ('sx', 'sy')), may hold values from -6 to 6
- source_count: int32 [2, 16], P('ev', ('sx', 'sy')), may hold values from 1 to 32, 392 in all within a row
Outputs:
- adjoint_final: float32 [2, 9, 32, 32, 128], P('ev', None, 'sx', 'sy')
- kernels: float32 [3, 32, 32, 128], P(None, 'sx', 'sy')
The draws below stay inside these ranges and needn't reach their ends.
Inputs may be any that keep to these rules, and one draw needn't show every extreme that they name: `station_block`: among the 32 rows of one device no block is named more than 16 times.
All inputs are finite; a program needn't handle non-finite values. No bound on the sum of `source_count` on one device may be relied on, other than what follows from the above.
Results may differ from the reference program's by a relative error of at most 0.0003.
Values sent between devices are 32-bit elements; how exact they have to be, the bound alone decides.
A program may use at most 64 MiB of HBM per device.

```python
import math
import jax
import jax.numpy as jnp
import numpy as np
from jax import lax

CX = 8
CY = 8
CZ = 128
STEPS = 3
S_DEV = 32
CAP = 16
EVENTS = 2
NX = 32
NY = 32
BLOCKS = 16
STATIONS = 512
N_SX = 4
N_SY = 4


def touch_ends(result, own_key, smallest, top_value):
    extent = result.shape
    index_at = [jax.random.randint(jax.random.fold_in(own_key, axis), (), 0, extent[axis]) for axis in range(len(extent))]
    result = result.at[tuple(index_at)].set(smallest)
    longest = extent.index(max(extent))
    index_at[longest] = (index_at[longest] + 1) % extent[longest]
    return result.at[tuple(index_at)].set(top_value)


def shard_levels(own_key, shape, split, smallest, top_value):
    def one(dim, parts):
        heights = jax.random.uniform(jax.random.fold_in(jax.random.fold_in(own_key, 6), dim), (parts,), jnp.float32, smallest / len(split), top_value / len(split))
        return jnp.repeat(jnp.exp(heights), shape[dim] // parts).reshape((-1,) + (1,) * (len(shape) - dim - 1))

    loudness = one(*split[0])
    for cut in split[1:]:
        loudness = loudness * one(*cut)
    return loudness


def profile(amount, total, most, lean):
    loads = [(1 << 20) // math.isqrt(rank ** lean) + 1 for rank in range(2, amount + 1)]
    spare, given = total - most - (amount - 1), [1] * (amount - 1)
    while spare > 0:
        movable = [i for i in range(amount - 1) if given[i] < most]
        whole, remaining = sum([loads[i] for i in movable]), spare
        for i in movable:
            extra = min(most - given[i], max(1, remaining * loads[i] // whole), spare)
            given[i] = given[i] + extra
            spare = spare - extra
    return np.array([most] + given)


def uneven(key, count, total, reach, slope):
    if count == 2:
        one = jax.random.randint(key, (), max(1, total - reach), min(reach, total - 1) + 1)
        return jnp.stack([one, total - one])
    sizes = jnp.asarray(profile(count, total, reach, slope), jnp.int32)
    pairs = (count - 1) // 2
    giver, taker = sizes[1:1 + 2 * pairs:2], sizes[2:2 + 2 * pairs:2]
    margin = jnp.minimum(giver - 1, reach - taker)
    passed = jax.random.randint(jax.random.fold_in(key, 1), (pairs,), 0, 1 << 20) % (margin + 1)
    sizes = sizes.at[1:1 + 2 * pairs:2].set(giver - passed).at[2:2 + 2 * pairs:2].set(taker + passed)
    return sizes[jax.random.permutation(jax.random.fold_in(key, 2), count)]


def shared_out(stream_key, own, number, rows, number_of, top, bound, skew):
    sequence = jax.random.permutation(stream_key, number_of)
    crowded, usual = portions_of(number_of, rows * top, bound, skew, True), portions_of(number_of, rows * top, bound, skew, False)
    places = jnp.arange(number_of)

    def named(lengths, offset_by):
        used = int((lengths > 0).sum())
        fixed = max(1, used // 4)
        moved = fixed + (places - fixed + offset_by * (used - fixed)) % max(1, number_of - fixed)
        return jnp.zeros((number_of,), jnp.int32).at[sequence[jnp.where(places < fixed, places, moved)]].set(jnp.asarray(lengths, jnp.int32))

    lengths = jnp.where(number % 4 == 0, named(crowded, number // 4), named(usual, number - number // 4 - 1))
    mixed = jax.random.permutation(jax.random.fold_in(own, 3), number_of)
    giver, receiver = mixed[0:number_of // 2 * 2:2], mixed[1:number_of // 2 * 2:2]
    slack = jnp.minimum(lengths[giver] - 1, bound - lengths[receiver]) // 2
    slack = jnp.where((giver == sequence[0]) | (receiver == sequence[0]) | (lengths[receiver] == 0), 0, jnp.maximum(slack, 0))
    moved = jax.random.randint(jax.random.fold_in(own, 4), (number_of // 2,), 0, 1 << 20) % (slack + 1)
    lengths = lengths.at[giver].add(-moved).at[receiver].add(moved)
    labels = jnp.searchsorted(jnp.cumsum(lengths), jnp.arange(rows * top), side="right").astype(jnp.int32)
    table = labels.reshape(top, rows).T
    table = table[jax.random.permutation(jax.random.fold_in(own, 1), rows)]
    offset_by = jax.random.randint(jax.random.fold_in(own, 2), (rows, 1), 0, top)
    return jnp.take_along_axis(table, (jnp.arange(top)[None, :] + offset_by) % top, axis=1)


def portions_of(count, total, bound, lean, full):
    loads = [(1 << 20) // math.isqrt(standing ** lean) + 1 for standing in range(1, count + 1)]
    largest = bound if full else min(bound, max(-(-total // count), total * loads[0] // sum(loads)))
    least = 1 if total - largest >= count - 1 else 0
    holding, spare = [largest] + [least] * (count - 1), total - largest - least * (count - 1)
    while spare > 0:
        free = [i for i in range(1, count) if holding[i] < largest] or [i for i in range(1, count) if holding[i] < bound]
        whole, left = sum([loads[i] for i in free]), spare
        for i in free:
            more = min(bound - holding[i], max(1, left * loads[i] // whole), spare)
            holding[i] = holding[i] + more
            spare = spare - more
    return np.array(holding)


def gaussian(own_key, dims, width, reach, shards=(), kind=jnp.bfloat16):
    result = jax.random.normal(own_key, dims, jnp.float32) * width
    if len(shards) > 0:
        result = shard_levels(own_key, dims, shards, -0.22, 0.18) * result
    return jnp.clip(result, min=-reach, max=reach).astype(kind)


def setup_inputs(seed: int = 0) -> dict:
    key_of = jax.random.split(jax.random.key(seed), 10)
    adjoint_state = gaussian(key_of[0], (EVENTS, 9, NX, NY, CZ), 1.0, 6.0, ((0, 2), (2, 4), (3, 4)), jnp.float32)
    forward_state = gaussian(key_of[1], (EVENTS, STEPS, 9, NX, NY, CZ), 1.0, 6.0, ((0, 2), (3, 4), (4, 4)))
    inv_density = jnp.clip(jnp.exp(math.log(1.6) - 0.98082923 * jax.random.uniform(key_of[2], (NX, NY, CZ), jnp.float32) ** shard_levels(key_of[2], (NX, NY, CZ), ((0, 4), (1, 4)), -0.2, 0.2)), 0.6, 1.6)
    lame_lambda = jnp.clip(jnp.exp(math.log(0.5) - 1.2039728 * jax.random.uniform(key_of[3], (NX, NY, CZ), jnp.float32) ** shard_levels(key_of[3], (NX, NY, CZ), ((0, 4), (1, 4)), -0.2, 0.2)), 0.15, 0.5)
    shear_modulus = jnp.clip(jnp.exp(math.log(0.4) - 1.3862944 * jax.random.uniform(key_of[4], (NX, NY, CZ), jnp.float32) ** shard_levels(key_of[4], (NX, NY, CZ), ((0, 4), (1, 4)), -0.2, 0.2)), 0.1, 0.4)
    station_block_keys = jax.random.split(jax.random.fold_in(key_of[5], 1), EVENTS * STATIONS // S_DEV)
    station_block_turns = jax.random.permutation(jax.random.fold_in(key_of[5], 3), EVENTS * STATIONS // S_DEV)
    station_block = jax.vmap(lambda own, number: shared_out(jax.random.fold_in(key_of[5], 2), own, number, S_DEV, N_SY, 1, CAP, 2))(station_block_keys, station_block_turns).reshape((EVENTS, STATIONS, 1))
    station_cell = touch_ends(jax.random.randint(key_of[6], (EVENTS, STATIONS), 0, CX * CY), jax.random.fold_in(key_of[6], 1), 0, (CX * CY) - 1).astype(jnp.int32)
    station_trace = gaussian(key_of[7], (EVENTS, STATIONS, 3 * STEPS), 1.0, 6.0, ((0, 2), (1, 16)), jnp.float32)
    source_count = jax.vmap(lambda own: uneven(own, BLOCKS, ((N_SX * N_SY - 1) * 3 * S_DEV) // 4 + S_DEV, S_DEV, 1))(jax.random.split(key_of[8], EVENTS)).reshape((EVENTS, BLOCKS)).astype(jnp.int32)
    return {"adjoint_state": adjoint_state, "forward_state": forward_state, "inv_density": inv_density, "lame_lambda": lame_lambda, "shear_modulus": shear_modulus, "station_block": station_block, "station_cell": station_cell, "station_trace": station_trace, "source_count": source_count}


DT = 0.35
stress_faces = ([0], [3, 4], [1], [3, 5])
velocity_faces = ([1, 2], [0], [0, 2], [1])


def shift_upper(field, axis, plane):
    size = field.shape[axis]
    inner = lax.slice_in_dim(field, 1, size, axis=axis)
    return jnp.concatenate([inner, plane], axis=axis)


def shift_lower(field, axis, plane):
    size = field.shape[axis]
    inner = lax.slice_in_dim(field, 0, size - 1, axis=axis)
    return jnp.concatenate([plane, inner], axis=axis)


def above_diff(field):
    zeros_plane = jnp.zeros(field.shape[:-1] + (1,), jnp.float32)
    return jnp.concatenate([field[..., 1:], zeros_plane], axis=-1) - field


def below_diff(field):
    zeros_plane = jnp.zeros(field.shape[:-1] + (1,), jnp.float32)
    return field - jnp.concatenate([zeros_plane, field[..., :-1]], axis=-1)


def accelerate(stress, planes, inv_density, force):
    high_x, low_x, high_y, low_y = planes
    next_x = shift_upper(stress[:, stress_faces[0]], 2, high_x)
    prev_x = shift_lower(stress[:, stress_faces[1]], 2, low_x)
    next_y = shift_upper(stress[:, stress_faces[2]], 3, high_y)
    prev_y = shift_lower(stress[:, stress_faces[3]], 3, low_y)
    sxx, syy, szz, sxy, sxz, syz = [stress[:, c] for c in range(6)]
    accel_x = (next_x[:, 0] - sxx) + (sxy - prev_y[:, 0]) + below_diff(sxz)
    accel_y = (sxy - prev_x[:, 0]) + (next_y[:, 0] - syy) + below_diff(syz)
    accel_z = (sxz - prev_x[:, 1]) + (syz - prev_y[:, 1]) + above_diff(szz)
    accel = jnp.stack([accel_x, accel_y, accel_z], axis=1)
    accel = accel.at[..., 0].add(force)
    return DT * inv_density * accel


def strain_rates(velocity, planes):
    high_x, low_x, high_y, low_y = planes
    next_x = shift_upper(velocity[:, velocity_faces[0]], 2, high_x)
    prev_x = shift_lower(velocity[:, velocity_faces[1]], 2, low_x)
    next_y = shift_upper(velocity[:, velocity_faces[2]], 3, high_y)
    prev_y = shift_lower(velocity[:, velocity_faces[3]], 3, low_y)
    vel_x, vel_y, vel_z = velocity[:, 0], velocity[:, 1], velocity[:, 2]
    rate_xx = vel_x - prev_x[:, 0]
    rate_yy = vel_y - prev_y[:, 0]
    rate_zz = below_diff(vel_z)
    rate_xy = 0.5 * ((next_y[:, 0] - vel_x) + (next_x[:, 0] - vel_y))
    rate_xz = 0.5 * (above_diff(vel_x) + (next_x[:, 1] - vel_z))
    rate_yz = 0.5 * (above_diff(vel_y) + (next_y[:, 1] - vel_z))
    return jnp.stack([rate_xx, rate_yy, rate_zz, rate_xy, rate_xz, rate_yz], axis=1)


def stress_update(stress, rates, lame_lambda, shear_modulus, strains):
    trace = rates[:, 0] + rates[:, 1] + rates[:, 2]
    diagonal = stress[:, :3] + DT * (lame_lambda * trace[:, None] + 2.0 * shear_modulus * rates[:, :3])
    offdiag = stress[:, 3:] + DT * 2.0 * shear_modulus * rates[:, 3:]
    forward_trace = strains[:, 0] + strains[:, 1] + strains[:, 2]
    lambda_term = DT * forward_trace * trace
    shear_term = DT * 2.0 * (jnp.sum(strains[:, :3] * rates[:, :3], axis=1) + 2.0 * jnp.sum(strains[:, 3:] * rates[:, 3:], axis=1))
    return jnp.concatenate([diagonal, offdiag], axis=1), lambda_term, shear_term


def zero_planes(stack, faces):
    events, comps, size_x, size_y, size_z = stack.shape
    return (jnp.zeros((events, len(faces[0]), 1, size_y, size_z), jnp.float32),
            jnp.zeros((events, len(faces[1]), 1, size_y, size_z), jnp.float32),
            jnp.zeros((events, len(faces[2]), size_x, 1, size_z), jnp.float32),
            jnp.zeros((events, len(faces[3]), size_x, 1, size_z), jnp.float32))


def reference(adjoint_state, forward_state, inv_density, lame_lambda, shear_modulus, station_block, station_cell, station_trace, source_count):
    stations = station_cell.shape[1]
    index = jnp.arange(stations, dtype=jnp.int32)
    owner = index // S_DEV
    within = index % S_DEV
    row_x = index // (N_SY * S_DEV)

    def one_event(event):
        state = adjoint_state[event][None]
        forward = forward_state[event][None]
        counts = source_count[event]
        live = (within < counts[owner]).astype(jnp.float32)
        cells = station_cell[event]
        grid_x = (row_x * CX + cells // CY).astype(jnp.int32)
        grid_y = (station_block[event, :, 0] * CY + cells % CY).astype(jnp.int32)
        traces = station_trace[event] * live[:, None]
        surface = jnp.zeros((NX, NY, 3 * STEPS), jnp.float32).at[grid_x, grid_y].add(traces)
        zero_k = jnp.zeros((1, NX, NY, CZ), jnp.float32)
        rho_kernel, lambda_kernel, shear_kernel = zero_k, zero_k, zero_k
        for step in range(STEPS):
            force = jnp.moveaxis(surface[:, :, 3 * step:3 * step + 3], 2, 0)[None]
            stress = state[:, 3:]
            change = accelerate(stress, zero_planes(stress, stress_faces), inv_density, force)
            velocity = state[:, :3] + change
            rho_kernel = rho_kernel + jnp.sum(forward[:, step, :3].astype(jnp.float32) * change, axis=1)
            rates = strain_rates(velocity, zero_planes(velocity, velocity_faces))
            stress, lambda_term, shear_term = stress_update(stress, rates, lame_lambda, shear_modulus, forward[:, step, 3:].astype(jnp.float32))
            lambda_kernel = lambda_kernel + lambda_term
            shear_kernel = shear_kernel + shear_term
            state = jnp.concatenate([velocity, stress], axis=1)
        return state[0], jnp.concatenate([rho_kernel, lambda_kernel, shear_kernel], axis=0)

    states, event_kernels = lax.map(one_event, jnp.arange(EVENTS, dtype=jnp.int32))
    return states, jnp.sum(event_kernels, axis=0)
```

```python
import functools

import jax
import jax.numpy as jnp
from jax import lax
from jax.experimental import pallas as pl
from jax.experimental.pallas import tpu as pltpu
from jax.sharding import PartitionSpec as P

DT = 0.35
MESH = pl.DeviceIdType.MESH

STRESS_FACES = ((3,), (6, 7), (4,), (6, 8))
VELOCITY_FACES = ((1, 2), (0,), (0, 2), (1,))


def kernel(
    n_sx, n_sy, n_ev, cx, cy, cz, steps, owned,
    adj, fwd, inv_density, lame, shear, blocks, cells, traces, counts,
    state, total,
    fwd_v, dens_v, lame_v, shear_v, blocks_v, cells_v, traces_v, counts_v,
    plane_out, plane_in, rows_out, rows_in, kern_in,
    load_sem, face_send, face_recv, rows_send, rows_recv, kern_send, kern_recv,
):
    ix, iy, ie = lax.axis_index("sx"), lax.axis_index("sy"), lax.axis_index("ev")
    area = cx * cy

    pairs = [
        (traces, traces_v), (blocks, blocks_v), (counts, counts_v), (cells, cells_v),
        (adj, state), (inv_density, dens_v), (fwd, fwd_v), (lame, lame_v), (shear, shear_v),
    ]
    loads = [pltpu.make_async_copy(a, b, load_sem.at[i]) for i, (a, b) in enumerate(pairs)]
    for load in loads:
        load.start()

    goes = (ix > 0, ix < n_sx - 1, iy > 0, iy < n_sy - 1)
    comes = (ix < n_sx - 1, ix > 0, iy < n_sy - 1, iy > 0)
    targets = ({"sx": ix - 1}, {"sx": ix + 1}, {"sy": iy - 1}, {"sy": iy + 1})

    barrier = pltpu.get_barrier_semaphore()
    for side in (0, 1):
        @pl.when(goes[side])
        def _(side=side):
            pl.semaphore_signal(barrier, inc=1, device_id=targets[side], device_id_type=MESH)
    for d in range(1, n_sy):
        pl.semaphore_signal(barrier, inc=1, device_id={"sy": lax.rem(iy + d, n_sy)}, device_id_type=MESH)
    for d in range(1, n_ev):
        pl.semaphore_signal(barrier, inc=1, device_id={"ev": lax.rem(ie + d, n_ev)}, device_id_type=MESH)

    for side in range(4):
        @pl.when(jnp.logical_not(comes[side]))
        def _(side=side):
            plane_in[:, side] = jnp.zeros((2 * steps, 2, max(cx, cy), cz), jnp.float32)

    for load in loads[:4]:
        load.wait()
    row = lax.broadcasted_iota(jnp.int32, (owned, 1), 0)
    live = row < counts_v[...]
    lanes_used = traces_v.shape[1]
    for d in range(n_sy):
        goal = lax.rem(iy + d, n_sy)
        keep = jnp.logical_and(live, blocks_v[...] == goal)
        rows_out[d, :owned, :] = jnp.zeros((owned, 128), jnp.float32)
        rows_out[d, :owned, :lanes_used] = jnp.where(keep, traces_v[...], 0.0)
        rows_out[d, owned:, :] = jnp.zeros((8, 128), jnp.float32)
        rows_out[d, owned:owned + 1, :owned] = cells_v[...].astype(jnp.float32)

    amount = (n_sy - 1) + (n_ev - 1) + (ix > 0).astype(jnp.int32) + (ix < n_sx - 1).astype(jnp.int32)
    pl.semaphore_wait(barrier, amount)

    def face_copy(turn, side, count):
        return pltpu.make_async_remote_copy(
            src_ref=plane_out.at[turn, side, pl.ds(0, count)],
            dst_ref=plane_in.at[turn, side, pl.ds(0, count)],
            send_sem=face_send.at[turn, side],
            recv_sem=face_recv.at[turn, side],
            device_id=targets[side],
            device_id_type=MESH,
        )

    def send_faces(turn, faces):
        for side, fields in enumerate(faces):
            for i, f in enumerate(fields):
                if side == 0:
                    plane_out[turn, side, i, :cy] = state[f, 0:cy, :]
                elif side == 1:
                    plane_out[turn, side, i, :cy] = state[f, area - cy:area, :]
                else:
                    at = 0 if side == 2 else cy - 1
                    plane_out[turn, side, i, :cx] = state[f, pl.ds(at, cx, stride=cy), :]

            @pl.when(goes[side])
            def _(side=side, fields=fields):
                face_copy(turn, side, len(fields)).start()

    def receive_faces(turn, faces):
        for side, fields in enumerate(faces):
            @pl.when(comes[side])
            def _(side=side, fields=fields):
                face_copy(turn, side, len(fields)).wait_recv()

    def rows_copy(d):
        return pltpu.make_async_remote_copy(
            src_ref=rows_out.at[d],
            dst_ref=rows_in.at[d - 1],
            send_sem=rows_send.at[d - 1],
            recv_sem=rows_recv.at[d - 1],
            device_id={"sy": lax.rem(iy + d, n_sy)},
            device_id_type=MESH,
        )

    def kern_copy(d, first, count, part):
        return pltpu.make_async_remote_copy(
            src_ref=total.at[pl.ds(first, count)],
            dst_ref=kern_in.at[d - 1, pl.ds(first, count)],
            send_sem=kern_send.at[d - 1, part],
            recv_sem=kern_recv.at[d - 1, part],
            device_id={"ev": lax.rem(ie + d, n_ev)},
            device_id_type=MESH,
        )

    loads[4].wait()
    send_faces(0, STRESS_FACES)
    for d in range(1, n_sy):
        rows_copy(d).start()
    for load in loads[5:]:
        load.wait()

    lane = lax.broadcasted_iota(jnp.int32, (area, cz), 1)
    y_at = lax.rem(lax.broadcasted_iota(jnp.int32, (area, cz), 0), cy)
    first_z, last_z = lane == 0, lane == cz - 1
    first_y, last_y = y_at == 0, y_at == cy - 1

    def above(f):
        return jnp.where(last_z, 0.0, pltpu.roll(f, cz - 1, 1))

    def below(f):
        return jnp.where(first_z, 0.0, pltpu.roll(f, 1, 1))

    def next_x(f, turn, i):
        return jnp.concatenate([f[cy:], plane_in[turn, 0, i, :cy]], axis=0)

    def prev_x(f, turn, i):
        return jnp.concatenate([plane_in[turn, 1, i, :cy], f[:area - cy]], axis=0)

    def spread(turn, side, i):
        return jnp.concatenate(
            [jnp.broadcast_to(plane_in[turn, side, i, x:x + 1], (cy, cz)) for x in range(cx)], axis=0
        )

    def next_y(f, turn, i):
        return jnp.where(last_y, spread(turn, 2, i), pltpu.roll(f, area - 1, 0))

    def prev_y(f, turn, i):
        return jnp.where(first_y, spread(turn, 3, i), pltpu.roll(f, 1, 0))

    def forward(step, f):
        return fwd_v[step, f].astype(jnp.float32).reshape(area, cz)

    def scattered(rows):
        cell = lax.broadcasted_iota(jnp.int32, (area, owned), 0).astype(jnp.float32)
        table = (cell == rows[owned:owned + 1, :owned]).astype(jnp.float32)
        return jnp.dot(
            table, rows[:owned, :], precision=lax.Precision.HIGHEST, preferred_element_type=jnp.float32
        )

    surface = scattered(rows_out.at[0])
    for d in range(1, n_sy):
        rows_copy(d).wait_recv()
        surface = surface + scattered(rows_in.at[d - 1])

    def force(k):
        moved = surface if k == 0 else pltpu.roll(surface, 128 - k, 1)
        return jnp.where(first_z, moved, 0.0)

    for step in range(steps):
        last = step == steps - 1
        turn = 2 * step
        forces = [force(3 * step + c) for c in range(3)]
        receive_faces(turn, STRESS_FACES)
        sxx, syy, szz, sxy, sxz, syz = [state[3 + c] for c in range(6)]
        accel_x = (next_x(sxx, turn, 0) - sxx) + (sxy - prev_y(sxy, turn, 0)) + (sxz - below(sxz))
        accel_y = (sxy - prev_x(sxy, turn, 0)) + (next_y(syy, turn, 0) - syy) + (syz - below(syz))
        accel_z = (sxz - prev_x(sxz, turn, 1)) + (syz - prev_y(syz, turn, 1)) + (above(szz) - szz)
        scale = DT * dens_v[...]
        change = [scale * (a + f) for a, f in zip((accel_x, accel_y, accel_z), forces)]
        for c in range(3):
            state[c] = state[c] + change[c]
        turn += 1
        send_faces(turn, VELOCITY_FACES)

        rho = sum(forward(step, c) * change[c] for c in range(3))
        total[0] = rho if step == 0 else total[0] + rho
        if last:
            for d in range(1, n_ev):
                kern_copy(d, 0, 1, 0).start()
        strain = [forward(step, 3 + c) for c in range(6)]

        receive_faces(turn, VELOCITY_FACES)
        vx, vy, vz = [state[c] for c in range(3)]
        exx = vx - prev_x(vx, turn, 0)
        eyy = vy - prev_y(vy, turn, 0)
        ezz = vz - below(vz)
        exy = 0.5 * ((next_y(vx, turn, 0) - vx) + (next_x(vy, turn, 0) - vy))
        exz = 0.5 * ((above(vx) - vx) + (next_x(vz, turn, 1) - vz))
        eyz = 0.5 * ((above(vy) - vy) + (next_y(vz, turn, 1) - vz))
        rates = (exx, eyy, ezz, exy, exz, eyz)
        trace = exx + eyy + ezz

        def update_stress():
            mu = (DT * 2.0) * shear_v[...]
            common = DT * lame_v[...] * trace
            for c in range(6):
                moved = mu * rates[c]
                state[3 + c] = state[3 + c] + (moved + common if c < 3 else moved)

        def update_kernels():
            lam = DT * (strain[0] + strain[1] + strain[2]) * trace
            diagonal = strain[0] * exx + strain[1] * eyy + strain[2] * ezz
            others = strain[3] * exy + strain[4] * exz + strain[5] * eyz
            she = (DT * 2.0) * (diagonal + 2.0 * others)
            total[1] = lam if step == 0 else total[1] + lam
            total[2] = she if step == 0 else total[2] + she

        if last:
            update_kernels()
            for d in range(1, n_ev):
                kern_copy(d, 1, 2, 1).start()
            update_stress()
        else:
            update_stress()
            send_faces(turn + 1, STRESS_FACES)
            update_kernels()

    for step in range(steps):
        for turn, faces in ((2 * step, STRESS_FACES), (2 * step + 1, VELOCITY_FACES)):
            for side, fields in enumerate(faces):
                @pl.when(goes[side])
                def _(turn=turn, side=side, fields=fields):
                    face_copy(turn, side, len(fields)).wait_send()
    for d in range(1, n_sy):
        rows_copy(d).wait_send()
    for d in range(1, n_ev):
        kern_copy(d, 0, 1, 0).wait()
        kern_copy(d, 1, 2, 1).wait()
    for c in range(3):
        value = total[c]
        for d in range(1, n_ev):
            value = value + kern_in[d - 1, c]
        total[c] = value


def on_device(
    sizes,
    adjoint_state,
    forward_state,
    inv_density,
    lame_lambda,
    shear_modulus,
    station_block,
    station_cell,
    station_trace,
    source_count,
):
    n_sx, n_sy, n_ev = sizes
    fields, cx, cy, cz = adjoint_state.shape[1:]
    steps = forward_state.shape[1]
    owned = station_cell.shape[1]
    area, wide = cx * cy, max(cx, cy)
    anywhere = pl.BlockSpec(memory_space=pl.ANY)
    vmem = pl.BlockSpec(memory_space=pltpu.VMEM)
    f32, i32 = jnp.float32, jnp.int32
    state, kernels = pl.pallas_call(
        functools.partial(kernel, n_sx, n_sy, n_ev, cx, cy, cz, steps, owned),
        out_shape=(
            jax.ShapeDtypeStruct((fields, area, cz), f32),
            jax.ShapeDtypeStruct((3, area, cz), f32),
        ),
        in_specs=[anywhere] * 9,
        out_specs=(vmem, vmem),
        scratch_shapes=[
            pltpu.VMEM((steps, fields, cx, cy, cz), jnp.bfloat16),
            pltpu.VMEM((area, cz), f32),
            pltpu.VMEM((area, cz), f32),
            pltpu.VMEM((area, cz), f32),
            pltpu.VMEM((owned, 1), i32),
            pltpu.VMEM((1, owned), i32),
            pltpu.VMEM((owned, 3 * steps), f32),
            pltpu.VMEM((1, 1), i32),
            pltpu.VMEM((2 * steps, 4, 2, wide, cz), f32),
            pltpu.VMEM((2 * steps, 4, 2, wide, cz), f32),
            pltpu.VMEM((n_sy, owned + 8, 128), f32),
            pltpu.VMEM((max(1, n_sy - 1), owned + 8, 128), f32),
            pltpu.VMEM((max(1, n_ev - 1), 3, area, cz), f32),
            pltpu.SemaphoreType.DMA((9,)),
            pltpu.SemaphoreType.DMA((2 * steps, 4)),
            pltpu.SemaphoreType.DMA((2 * steps, 4)),
            pltpu.SemaphoreType.DMA((max(1, n_sy - 1),)),
            pltpu.SemaphoreType.DMA((max(1, n_sy - 1),)),
            pltpu.SemaphoreType.DMA((max(1, n_ev - 1), 2)),
            pltpu.SemaphoreType.DMA((max(1, n_ev - 1), 2)),
        ],
        compiler_params=pltpu.CompilerParams(
            collective_id=0, has_side_effects=True, vmem_limit_bytes=24 * 1024 * 1024
        ),
    )(
        adjoint_state.reshape(fields, area, cz),
        forward_state[0],
        inv_density.reshape(area, cz),
        lame_lambda.reshape(area, cz),
        shear_modulus.reshape(area, cz),
        station_block[0],
        station_cell,
        station_trace[0],
        source_count,
    )
    return state.reshape(1, fields, cx, cy, cz), kernels.reshape(3, cx, cy, cz)


def solution(mesh):
    sizes = tuple(mesh.shape[name] for name in ("sx", "sy", "ev"))
    return jax.shard_map(
        functools.partial(on_device, sizes),
        mesh=mesh,
        in_specs=(
            P("ev", None, "sx", "sy", None),
            P("ev", None, None, "sx", "sy", None),
            P("sx", "sy", None),
            P("sx", "sy", None),
            P("sx", "sy", None),
            P("ev", ("sx", "sy"), None),
            P("ev", ("sx", "sy")),
            P("ev", ("sx", "sy"), None),
            P("ev", ("sx", "sy")),
        ),
        out_specs=(P("ev", None, "sx", "sy", None), P(None, "sx", "sy", None)),
        check_vma=False,
    )
```

```python
import functools

import jax
import jax.numpy as jnp
from jax import lax
from jax.experimental import pallas as pl
from jax.experimental.pallas import tpu as pltpu
from jax.sharding import PartitionSpec as P

DT = 0.35
MESH = pl.DeviceIdType.MESH

STRESS_FACES = ((3,), (6, 7), (4,), (6, 8))
VELOCITY_FACES = ((1, 2), (0,), (0, 2), (1,))


def kernel(
    n_sx, n_sy, n_ev, cx, cy, cz, steps, owned,
    adj, fwd, inv_density, lame, shear, blocks, cells, traces, counts,
    state_out, total_out,
    state, total, forces, fwd_v, dens_v, lame_v, shear_v, blocks_v, cells_v, traces_v,
    plane_out, plane_in, corner_out, corner_in, rows_out, rows_in, kern_in,
    load_sem, store_sem, face_send, face_recv, corner_send, corner_recv, rows_send, rows_recv, kern_send, kern_recv,
):
    ix, iy, ie = lax.axis_index("sx"), lax.axis_index("sy"), lax.axis_index("ev")
    area = cx * cy

    pairs = [
        (traces, traces_v), (blocks, blocks_v), (cells, cells_v),
        (inv_density, dens_v), (adj, state), (fwd, fwd_v), (lame, lame_v), (shear, shear_v),
    ]
    loads = [pltpu.make_async_copy(a, b, load_sem.at[i]) for i, (a, b) in enumerate(pairs)]
    for load in loads:
        load.start()

    goes = (ix > 0, ix < n_sx - 1, iy > 0, iy < n_sy - 1)
    comes = (ix < n_sx - 1, ix > 0, iy < n_sy - 1, iy > 0)
    targets = ({"sx": ix - 1}, {"sx": ix + 1}, {"sy": iy - 1}, {"sy": iy + 1})
    corners = ((0, 2), (0, 3), (1, 2), (1, 3))
    corner_goes = [jnp.logical_and(goes[a], goes[b]) for a, b in corners]
    corner_comes = [jnp.logical_and(comes[a], comes[b]) for a, b in corners]
    corner_targets = [{**targets[a], **targets[b]} for a, b in corners]
    turns = steps + 1

    barrier = pltpu.get_barrier_semaphore()
    for side in (0, 1):
        @pl.when(goes[side])
        def _(side=side):
            pl.semaphore_signal(barrier, inc=1, device_id=targets[side], device_id_type=MESH)
    for g in range(4):
        @pl.when(corner_goes[g])
        def _(g=g):
            pl.semaphore_signal(barrier, inc=1, device_id=corner_targets[g], device_id_type=MESH)
    for d in range(1, n_sy):
        pl.semaphore_signal(barrier, inc=1, device_id={"sy": lax.rem(iy + d, n_sy)}, device_id_type=MESH)
    for d in range(1, n_ev):
        pl.semaphore_signal(barrier, inc=1, device_id={"ev": lax.rem(ie + d, n_ev)}, device_id_type=MESH)

    for side in range(4):
        @pl.when(jnp.logical_not(comes[side]))
        def _(side=side):
            plane_in[:, side] = jnp.zeros((turns, 3, max(cx, cy), cz), jnp.float32)
    for g in range(4):
        @pl.when(jnp.logical_not(corner_comes[g]))
        def _(g=g):
            corner_in[:, g] = jnp.zeros((turns, 8, cz), jnp.float32)
    corner_out[...] = jnp.zeros(corner_out.shape, jnp.float32)

    for load in loads[:3]:
        load.wait()
    comps = 3 * steps
    live = lax.broadcasted_iota(jnp.int32, (1, owned), 1) < counts[0, 0]
    for d in range(n_sy):
        goal = lax.rem(iy + d, n_sy)
        keep = jnp.logical_and(live, blocks_v[0] == goal)
        for k in range(comps):
            rows_out[d, k:k + 1, :owned] = jnp.where(keep, traces_v[k], 0.0)
        rows_out[d, comps:comps + 1, :owned] = cells_v[...].astype(jnp.float32)

    amount = (n_sy - 1) + (n_ev - 1) + (ix > 0).astype(jnp.int32) + (ix < n_sx - 1).astype(jnp.int32)
    for g in range(4):
        amount = amount + corner_goes[g].astype(jnp.int32)
    pl.semaphore_wait(barrier, amount)

    def face_copy(turn, side, count):
        return pltpu.make_async_remote_copy(
            src_ref=plane_out.at[turn, side, pl.ds(0, count)],
            dst_ref=plane_in.at[turn, side, pl.ds(0, count)],
            send_sem=face_send.at[turn, side],
            recv_sem=face_recv.at[turn, side],
            device_id=targets[side],
            device_id_type=MESH,
        )

    def corner_copy(turn, g):
        return pltpu.make_async_remote_copy(
            src_ref=corner_out.at[turn, g],
            dst_ref=corner_in.at[turn, g],
            send_sem=corner_send.at[turn, g],
            recv_sem=corner_recv.at[turn, g],
            device_id=corner_targets[g],
            device_id_type=MESH,
        )

    def edge(ref, side):
        if side == 0:
            return ref[0:cy, :]
        if side == 1:
            return ref[area - cy:area, :]
        return ref[pl.ds(0 if side == 2 else cy - 1, cx, stride=cy), :]

    def send_faces(turn, planes):
        for side, values in enumerate(planes):
            for i, value in enumerate(values):
                plane_out[turn, side, i, :value.shape[0]] = value

            @pl.when(goes[side])
            def _(side=side, count=len(values)):
                face_copy(turn, side, count).start()

    def receive_faces(turn, counts):
        for side in range(4):
            @pl.when(comes[side])
            def _(side=side):
                face_copy(turn, side, counts[side]).wait_recv()

    def send_corners(turn):
        for g, at, fields in ((0, 0, (4, 3)), (1, cy - 1, (8,)), (2, area - cy, (7,)), (3, area - 1, (6,))):
            for i, f in enumerate(fields):
                corner_out[turn, g, i:i + 1] = state[f, at:at + 1, :]

            @pl.when(corner_goes[g])
            def _(g=g):
                corner_copy(turn, g).start()

    def receive_corners(turn):
        for g in range(4):
            @pl.when(corner_comes[g])
            def _(g=g):
                corner_copy(turn, g).wait_recv()

    def rows_copy(d):
        return pltpu.make_async_remote_copy(
            src_ref=rows_out.at[d],
            dst_ref=rows_in.at[d - 1],
            send_sem=rows_send.at[d - 1],
            recv_sem=rows_recv.at[d - 1],
            device_id={"sy": lax.rem(iy + d, n_sy)},
            device_id_type=MESH,
        )

    def store(first, count, part):
        fields = pl.ds(first, count)
        return pltpu.make_async_copy(state.at[fields], state_out.at[fields], store_sem.at[part])

    def kern_copy(d, first, count, part):
        return pltpu.make_async_remote_copy(
            src_ref=total.at[pl.ds(first, count)],
            dst_ref=kern_in.at[d - 1, pl.ds(first, count)],
            send_sem=kern_send.at[d - 1, part],
            recv_sem=kern_recv.at[d - 1, part],
            device_id={"ev": lax.rem(ie + d, n_ev)},
            device_id_type=MESH,
        )

    loads[3].wait()
    loads[4].wait()
    send_faces(
        0,
        [[edge(state.at[f], side) for f in STRESS_FACES[side]] + [DT * edge(dens_v, side)] for side in range(4)],
    )
    for d in range(1, n_sy):
        rows_copy(d).start()
    for load in loads[5:]:
        load.wait()

    lane = lax.broadcasted_iota(jnp.int32, (area, cz), 1)
    y_at = lax.rem(lax.broadcasted_iota(jnp.int32, (area, cz), 0), cy)
    first_z, last_z = lane == 0, lane == cz - 1
    first_y, last_y = y_at == 0, y_at == cy - 1

    def above(f):
        return jnp.where(last_z[:f.shape[0]], 0.0, pltpu.roll(f, cz - 1, 1))

    def below(f):
        return jnp.where(first_z[:f.shape[0]], 0.0, pltpu.roll(f, 1, 1))

    def next_x(f, plane):
        return jnp.concatenate([f[cy:], plane], axis=0)

    def prev_x(f, plane):
        return jnp.concatenate([plane, f[:area - cy]], axis=0)

    def spread(plane):
        return jnp.concatenate([jnp.broadcast_to(plane[x:x + 1], (cy, cz)) for x in range(cx)], axis=0)

    def next_y(f, plane):
        return jnp.where(last_y, spread(plane), pltpu.roll(f, area - 1, 0))

    def prev_y(f, plane):
        return jnp.where(first_y, spread(plane), pltpu.roll(f, 1, 0))

    def up(plane):
        size = plane.shape[0]
        at = lax.broadcasted_iota(jnp.int32, plane.shape, 0)
        return jnp.where(at == size - 1, 0.0, pltpu.roll(plane, size - 1, 0))

    def down(plane):
        at = lax.broadcasted_iota(jnp.int32, plane.shape, 0)
        return jnp.where(at == 0, 0.0, pltpu.roll(plane, 1, 0))

    def on_row(row, at, size):
        place = lax.broadcasted_iota(jnp.int32, (size, cz), 0)
        return jnp.where(place == at, jnp.broadcast_to(row, (size, cz)), 0.0)

    def received(turn, side, i):
        return plane_in[turn, side, i, :cy if side < 2 else cx]

    def advanced(step):
        planes = []
        for side in range(4):
            vx, vy, vz, sxx, syy, szz, sxy, sxz, syz = [edge(state.at[f], side) for f in range(9)]
            fx, fy, fz = [edge(forces.at[3 * step + c], side) for c in range(3)]
            scale = DT * edge(dens_v, side)
            if side == 0:
                y = vy + scale * (sxy + (up(syy) - syy) + (syz - below(syz)) + fy)
                z = vz + scale * (sxz + (syz - down(syz)) + (above(szz) - szz) + fz)
                planes.append([sxx, y, z])
            elif side == 1:
                x = vx + scale * ((sxy - down(sxy)) - sxx + (sxz - below(sxz)) + fx)
                planes.append([sxy, sxz, x])
            elif side == 2:
                x = vx + scale * ((up(sxx) - sxx) + sxy + (sxz - below(sxz)) + fx)
                z = vz + scale * ((sxz - down(sxz)) + syz + (above(szz) - szz) + fz)
                planes.append([syy, x, z])
            else:
                y = vy + scale * ((sxy - down(sxy)) - syy + (syz - below(syz)) + fy)
                planes.append([sxy, syz, y])
        return planes

    def completed(turn):
        dens = [received(0, side, len(STRESS_FACES[side])) for side in range(4)]
        far_syy, far_sxx = corner_in[turn, 0, 0:1], corner_in[turn, 0, 1:2]
        far_syz, far_sxz, far_sxy = corner_in[turn, 1, 0:1], corner_in[turn, 2, 0:1], corner_in[turn, 3, 0:1]
        high_x = (
            received(turn, 0, 1) + dens[0] * (on_row(far_syy, cy - 1, cy) - edge(state.at[6], 1)),
            received(turn, 0, 2) - dens[0] * (on_row(far_syz, 0, cy) + edge(state.at[7], 1)),
        )
        low_x = (received(turn, 1, 2) + dens[1] * (edge(state.at[3], 0) - on_row(far_sxy, 0, cy)),)
        high_y = (
            received(turn, 2, 1) + dens[2] * (on_row(far_sxx, cx - 1, cx) - edge(state.at[6], 3)),
            received(turn, 2, 2) - dens[2] * (on_row(far_sxz, 0, cx) + edge(state.at[8], 3)),
        )
        low_y = (received(turn, 3, 2) + dens[3] * (edge(state.at[4], 2) - on_row(far_sxy, 0, cx)),)
        return high_x, low_x, high_y, low_y

    def forward(step, f):
        return fwd_v[step, f].astype(jnp.float32).reshape(area, cz)

    cell = lax.broadcasted_iota(jnp.int32, (area, owned), 0).astype(jnp.float32)

    def sources():
        return [rows_out.at[0]] + [rows_in.at[d - 1] for d in range(1, n_sy)]

    def force(k):
        spread_out = sum(
            jnp.where(cell == rows[comps:comps + 1, :owned], rows[k:k + 1, :owned], 0.0) for rows in sources()
        )
        at_cell = jnp.sum(spread_out, axis=1, keepdims=True)
        return jnp.where(first_z, at_cell, 0.0)

    for d in range(1, n_sy):
        rows_copy(d).wait_recv()

    for c in range(3):
        forces[c] = force(c)
    first_counts = [len(faces) + 1 for faces in STRESS_FACES]
    velocity_counts = [len(faces) for faces in VELOCITY_FACES]
    late_counts = (3, 3, 3, 3)

    for step in range(steps):
        last = step == steps - 1
        turn = 0 if step == 0 else step + 1
        receive_faces(turn, first_counts if step == 0 else late_counts)
        if step > 0:
            receive_corners(turn)
            beside = completed(turn)
        sxx, syy, szz, sxy, sxz, syz = [state[3 + c] for c in range(6)]
        low_sxy, low_sxz = received(turn, 1, 0), received(turn, 1, 1)
        near_sxy, near_syz = received(turn, 3, 0), received(turn, 3, 1)
        accel_x = (next_x(sxx, received(turn, 0, 0)) - sxx) + (sxy - prev_y(sxy, near_sxy)) + (sxz - below(sxz))
        accel_y = (sxy - prev_x(sxy, low_sxy)) + (next_y(syy, received(turn, 2, 0)) - syy) + (syz - below(syz))
        accel_z = (sxz - prev_x(sxz, low_sxz)) + (syz - prev_y(syz, near_syz)) + (above(szz) - szz)
        scale = DT * dens_v[...]
        change = [scale * (a + forces[3 * step + c]) for c, a in enumerate((accel_x, accel_y, accel_z))]
        for c in range(3):
            state[c] = state[c] + change[c]
        if step == 0:
            send_faces(1, [[edge(state.at[f], side) for f in VELOCITY_FACES[side]] for side in range(4)])
            for k in range(3, comps):
                forces[k] = force(k)

        rho = sum(forward(step, c) * change[c] for c in range(3))
        total[0] = rho if step == 0 else total[0] + rho
        if last:
            for d in range(1, n_ev):
                kern_copy(d, 0, 1, 0).start()
        strain = [forward(step, 3 + c) for c in range(6)]

        if last:
            store(0, 3, 0).start()
        if step == 0:
            receive_faces(1, velocity_counts)
            beside = [[received(1, side, i) for i in range(velocity_counts[side])] for side in range(4)]
        high_x, low_x, high_y, low_y = beside
        vx, vy, vz = [state[c] for c in range(3)]
        exx = vx - prev_x(vx, low_x[0])
        eyy = vy - prev_y(vy, low_y[0])
        ezz = vz - below(vz)
        exy = 0.5 * ((next_y(vx, high_y[0]) - vx) + (next_x(vy, high_x[0]) - vy))
        exz = 0.5 * ((above(vx) - vx) + (next_x(vz, high_x[1]) - vz))
        eyz = 0.5 * ((above(vy) - vy) + (next_y(vz, high_y[1]) - vz))
        rates = (exx, eyy, ezz, exy, exz, eyz)
        trace = exx + eyy + ezz

        def update_stress():
            mu = (DT * 2.0) * shear_v[...]
            common = DT * lame_v[...] * trace
            for c in range(6):
                moved = mu * rates[c]
                state[3 + c] = state[3 + c] + (moved + common if c < 3 else moved)

        def update_kernels():
            lam = DT * (strain[0] + strain[1] + strain[2]) * trace
            diagonal = strain[0] * exx + strain[1] * eyy + strain[2] * ezz
            others = strain[3] * exy + strain[4] * exz + strain[5] * eyz
            she = (DT * 2.0) * (diagonal + 2.0 * others)
            total[1] = lam if step == 0 else total[1] + lam
            total[2] = she if step == 0 else total[2] + she

        if last:
            update_kernels()
            for d in range(1, n_ev):
                kern_copy(d, 1, 2, 1).start()
            update_stress()
            store(3, 6, 1).start()
        else:
            update_stress()
            send_faces(step + 2, advanced(step + 1))
            send_corners(step + 2)
            update_kernels()

    for turn in range(turns):
        sent = first_counts if turn == 0 else velocity_counts if turn == 1 else late_counts
        for side in range(4):
            @pl.when(goes[side])
            def _(turn=turn, side=side, count=sent[side]):
                face_copy(turn, side, count).wait_send()
        if turn > 1:
            for g in range(4):
                @pl.when(corner_goes[g])
                def _(turn=turn, g=g):
                    corner_copy(turn, g).wait_send()
    for d in range(1, n_sy):
        rows_copy(d).wait_send()
    for d in range(1, n_ev):
        kern_copy(d, 0, 1, 0).wait()
        kern_copy(d, 1, 2, 1).wait()
    for c in range(3):
        value = total[c]
        for d in range(1, n_ev):
            value = value + kern_in[d - 1, c]
        total[c] = value
    finish = pltpu.make_async_copy(total, total_out, store_sem.at[2])
    finish.start()
    store(0, 3, 0).wait()
    store(3, 6, 1).wait()
    finish.wait()


def on_device(
    sizes,
    adjoint_state,
    forward_state,
    inv_density,
    lame_lambda,
    shear_modulus,
    station_block,
    station_cell,
    station_trace,
    source_count,
):
    n_sx, n_sy, n_ev = sizes
    fields, cx, cy, cz = adjoint_state.shape[1:]
    steps = forward_state.shape[1]
    owned = station_cell.shape[1]
    area, wide = cx * cy, max(cx, cy)
    hbm = pl.BlockSpec(memory_space=pl.ANY)
    lines = -(-(3 * steps + 1) // 8) * 8
    f32, i32 = jnp.float32, jnp.int32
    state, kernels = pl.pallas_call(
        functools.partial(kernel, n_sx, n_sy, n_ev, cx, cy, cz, steps, owned),
        out_shape=(
            jax.ShapeDtypeStruct((fields, area, cz), f32),
            jax.ShapeDtypeStruct((3, area, cz), f32),
        ),
        in_specs=[hbm] * 8 + [pl.BlockSpec(memory_space=pltpu.SMEM)],
        out_specs=(hbm, hbm),
        scratch_shapes=[
            pltpu.VMEM((fields, area, cz), f32),
            pltpu.VMEM((3, area, cz), f32),
            pltpu.VMEM((3 * steps, area, cz), f32),
            pltpu.VMEM((steps, fields, cx, cy, cz), jnp.bfloat16),
            pltpu.VMEM((area, cz), f32),
            pltpu.VMEM((area, cz), f32),
            pltpu.VMEM((area, cz), f32),
            pltpu.VMEM((1, 1, owned), i32),
            pltpu.VMEM((1, owned), i32),
            pltpu.VMEM((3 * steps, 1, owned), f32),
            pltpu.VMEM((steps + 1, 4, 3, wide, cz), f32),
            pltpu.VMEM((steps + 1, 4, 3, wide, cz), f32),
            pltpu.VMEM((steps + 1, 4, 8, cz), f32),
            pltpu.VMEM((steps + 1, 4, 8, cz), f32),
            pltpu.VMEM((n_sy, lines, 128), f32),
            pltpu.VMEM((max(1, n_sy - 1), lines, 128), f32),
            pltpu.VMEM((max(1, n_ev - 1), 3, area, cz), f32),
            pltpu.SemaphoreType.DMA((8,)),
            pltpu.SemaphoreType.DMA((3,)),
            pltpu.SemaphoreType.DMA((steps + 1, 4)),
            pltpu.SemaphoreType.DMA((steps + 1, 4)),
            pltpu.SemaphoreType.DMA((steps + 1, 4)),
            pltpu.SemaphoreType.DMA((steps + 1, 4)),
            pltpu.SemaphoreType.DMA((max(1, n_sy - 1),)),
            pltpu.SemaphoreType.DMA((max(1, n_sy - 1),)),
            pltpu.SemaphoreType.DMA((max(1, n_ev - 1), 2)),
            pltpu.SemaphoreType.DMA((max(1, n_ev - 1), 2)),
        ],
        compiler_params=pltpu.CompilerParams(
            collective_id=0, has_side_effects=True, vmem_limit_bytes=60 * 1024 * 1024
        ),
    )(
        adjoint_state.reshape(fields, area, cz),
        forward_state[0],
        inv_density.reshape(area, cz),
        lame_lambda.reshape(area, cz),
        shear_modulus.reshape(area, cz),
        station_block.transpose(0, 2, 1),
        station_cell,
        station_trace.transpose(2, 0, 1),
        source_count,
    )
    return state.reshape(1, fields, cx, cy, cz), kernels.reshape(3, cx, cy, cz)


def solution(mesh):
    sizes = tuple(mesh.shape[name] for name in ("sx", "sy", "ev"))
    return jax.shard_map(
        functools.partial(on_device, sizes),
        mesh=mesh,
        in_specs=(
            P("ev", None, "sx", "sy", None),
            P("ev", None, None, "sx", "sy", None),
            P("sx", "sy", None),
            P("sx", "sy", None),
            P("sx", "sy", None),
            P("ev", ("sx", "sy"), None),
            P("ev", ("sx", "sy")),
            P("ev", ("sx", "sy"), None),
            P("ev", ("sx", "sy")),
        ),
        out_specs=(P("ev", None, "sx", "sy", None), P(None, "sx", "sy", None)),
        check_vma=False,
    )
```

```python
import functools

import jax
import jax.numpy as jnp
from jax import lax
from jax.experimental import pallas as pl
from jax.experimental.pallas import tpu as pltpu
from jax.sharding import PartitionSpec as P

DT = 0.35
MESH = pl.DeviceIdType.MESH


def kernel(
    n_sx, n_sy, n_ev, cx, cy, cz, steps, owned,
    adj, fwd, inv_density, lame, shear, blocks, cells, traces, counts,
    state, total,
    forces, fwd_v, dens_v, lame_v, shear_v, blocks_v, cells_v, traces_v,
    plane_out, plane_in, corner_out, corner_in, rows_out, rows_in, kern_in,
    load_sem, face_send, face_recv, corner_send, corner_recv, rows_send, rows_recv, kern_send, kern_recv,
):
    ix, iy, ie = lax.axis_index("sx"), lax.axis_index("sy"), lax.axis_index("ev")
    area = cx * cy

    pairs = [
        (traces, traces_v), (blocks, blocks_v), (cells, cells_v),
        (inv_density, dens_v), (adj, state), (fwd, fwd_v), (lame, lame_v), (shear, shear_v),
    ]
    loads = [pltpu.make_async_copy(a, b, load_sem.at[i]) for i, (a, b) in enumerate(pairs)]
    goes = (ix > 0, ix < n_sx - 1, iy > 0, iy < n_sy - 1)
    comes = (ix < n_sx - 1, ix > 0, iy < n_sy - 1, iy > 0)
    targets = ({"sx": ix - 1}, {"sx": ix + 1}, {"sy": iy - 1}, {"sy": iy + 1})
    corners = ((0, 2), (0, 3), (1, 2), (1, 3))
    corner_goes = [jnp.logical_and(goes[a], goes[b]) for a, b in corners]
    corner_comes = [jnp.logical_and(comes[a], comes[b]) for a, b in corners]
    corner_targets = [{**targets[a], **targets[b]} for a, b in corners]

    barrier = pltpu.get_barrier_semaphore()
    for side in (0, 1):
        @pl.when(goes[side])
        def _(side=side):
            for y in range(n_sy):
                where = {**targets[side], "sy": y}
                pl.semaphore_signal(barrier, inc=1, device_id=where, device_id_type=MESH)
    for d in range(1, n_sy):
        pl.semaphore_signal(barrier, inc=1, device_id={"sy": lax.rem(iy + d, n_sy)}, device_id_type=MESH)
    for d in range(1, n_ev):
        pl.semaphore_signal(barrier, inc=1, device_id={"ev": lax.rem(ie + d, n_ev)}, device_id_type=MESH)

    for load in loads:
        load.start()

    for side in range(4):
        @pl.when(jnp.logical_not(comes[side]))
        def _(side=side):
            plane_in[:, side] = jnp.zeros((steps, 4, max(cx, cy), cz), jnp.float32)
    for g in range(4):
        @pl.when(jnp.logical_not(corner_comes[g]))
        def _(g=g):
            corner_in[:, g] = jnp.zeros((steps, 8, cz), jnp.float32)
    for side in (0, 1):
        @pl.when(jnp.logical_not(comes[side]))
        def _(side=side):
            rows_in[1 + side] = jnp.zeros(rows_in.shape[1:], jnp.float32)
    corner_out[...] = jnp.zeros(corner_out.shape, jnp.float32)

    for load in loads[:3]:
        load.wait()
    comps = 3 * steps
    live = lax.broadcasted_iota(jnp.int32, (1, owned), 1) < counts[0, 0]
    for k in range(comps):
        rows_out[k:k + 1, :owned] = jnp.where(live, traces_v[k], 0.0)
    rows_out[comps:comps + 1, :owned] = (blocks_v[0] * area + cells_v[...]).astype(jnp.float32)

    across = n_sy * ((ix > 0).astype(jnp.int32) + (ix < n_sx - 1).astype(jnp.int32))
    pl.semaphore_wait(barrier, (n_sy - 1) + (n_ev - 1) + across)

    def face_copy(turn, side, count):
        return pltpu.make_async_remote_copy(
            src_ref=plane_out.at[turn, side, pl.ds(0, count)],
            dst_ref=plane_in.at[turn, side, pl.ds(0, count)],
            send_sem=face_send.at[turn, side],
            recv_sem=face_recv.at[turn, side],
            device_id=targets[side],
            device_id_type=MESH,
        )

    def corner_copy(turn, g):
        return pltpu.make_async_remote_copy(
            src_ref=corner_out.at[turn, g],
            dst_ref=corner_in.at[turn, g],
            send_sem=corner_send.at[turn, g],
            recv_sem=corner_recv.at[turn, g],
            device_id=corner_targets[g],
            device_id_type=MESH,
        )

    def edge(ref, side):
        if side == 0:
            return ref[0:cy, :]
        if side == 1:
            return ref[area - cy:area, :]
        return ref[pl.ds(0 if side == 2 else cy - 1, cx, stride=cy), :]

    def send_faces(turn, planes):
        for side, values in enumerate(planes):
            for i, value in enumerate(values):
                plane_out[turn, side, i, :value.shape[0]] = value

            @pl.when(goes[side])
            def _(side=side, count=len(values)):
                face_copy(turn, side, count).start()

    def receive_faces(turn, counts):
        for side in range(4):
            @pl.when(comes[side])
            def _(side=side):
                face_copy(turn, side, counts[side]).wait_recv()

    def send_corners(turn):
        for g, at, fields in ((0, 0, (4, 3)), (1, cy - 1, (8,)), (2, area - cy, (7,)), (3, area - 1, (6,))):
            for i, f in enumerate(fields):
                corner_out[turn, g, i:i + 1] = state[f, at:at + 1, :]

            @pl.when(corner_goes[g])
            def _(g=g):
                corner_copy(turn, g).start()

    def receive_corners(turn):
        for g in range(4):
            @pl.when(corner_comes[g])
            def _(g=g):
                corner_copy(turn, g).wait_recv()

    def rows_copy(line, d):
        where = {"sy": lax.rem(iy + d, n_sy)}
        return pltpu.make_async_remote_copy(
            src_ref=rows_out,
            dst_ref=rows_in.at[line, d],
            send_sem=rows_send.at[line, d],
            recv_sem=rows_recv.at[line, d],
            device_id={**targets[line - 1], **where} if line else where,
            device_id_type=MESH,
        )

    def kern_copy(d, first, count, part):
        return pltpu.make_async_remote_copy(
            src_ref=total.at[pl.ds(first, count)],
            dst_ref=kern_in.at[d - 1, pl.ds(first, count)],
            send_sem=kern_send.at[d - 1, part],
            recv_sem=kern_recv.at[d - 1, part],
            device_id={"ev": lax.rem(ie + d, n_ev)},
            device_id_type=MESH,
        )

    lane = lax.broadcasted_iota(jnp.int32, (area, cz), 1)
    y_at = lax.rem(lax.broadcasted_iota(jnp.int32, (area, cz), 0), cy)
    first_z, last_z = lane == 0, lane == cz - 1
    first_y, last_y = y_at == 0, y_at == cy - 1

    def above(f):
        return jnp.where(last_z[:f.shape[0]], 0.0, pltpu.roll(f, cz - 1, 1))

    def below(f):
        return jnp.where(first_z[:f.shape[0]], 0.0, pltpu.roll(f, 1, 1))

    def next_x(f, plane):
        return jnp.concatenate([f[cy:], plane], axis=0)

    def prev_x(f, plane):
        return jnp.concatenate([plane, f[:area - cy]], axis=0)

    def spread(plane):
        return jnp.concatenate([jnp.broadcast_to(plane[x:x + 1], (cy, cz)) for x in range(cx)], axis=0)

    def next_y(f, plane):
        return jnp.where(last_y, spread(plane), pltpu.roll(f, area - 1, 0))

    def prev_y(f, plane):
        return jnp.where(first_y, spread(plane), pltpu.roll(f, 1, 0))

    def up(plane):
        size = plane.shape[0]
        at = lax.broadcasted_iota(jnp.int32, plane.shape, 0)
        return jnp.where(at == size - 1, 0.0, pltpu.roll(plane, size - 1, 0))

    def down(plane):
        at = lax.broadcasted_iota(jnp.int32, plane.shape, 0)
        return jnp.where(at == 0, 0.0, pltpu.roll(plane, 1, 0))

    def on_row(row, at, size):
        place = lax.broadcasted_iota(jnp.int32, (size, cz), 0)
        return jnp.where(place == at, jnp.broadcast_to(row, (size, cz)), 0.0)

    def received(turn, side, i):
        return plane_in[turn, side, i, :cy if side < 2 else cx]

    def advanced(step, with_force=True):
        planes = []
        for side in range(4):
            vx, vy, vz, sxx, syy, szz, sxy, sxz, syz = [edge(state.at[f], side) for f in range(9)]
            fx, fy, fz = [edge(forces.at[3 * step + c], side) if with_force else 0.0 for c in range(3)]
            scale = DT * edge(dens_v, side)
            if side == 0:
                y = vy + scale * (sxy + (up(syy) - syy) + (syz - below(syz)) + fy)
                z = vz + scale * (sxz + (syz - down(syz)) + (above(szz) - szz) + fz)
                planes.append([sxx, y, z])
            elif side == 1:
                x = vx + scale * ((sxy - down(sxy)) - sxx + (sxz - below(sxz)) + fx)
                planes.append([sxy, sxz, x])
            elif side == 2:
                x = vx + scale * ((up(sxx) - sxx) + sxy + (sxz - below(sxz)) + fx)
                z = vz + scale * ((sxz - down(sxz)) + syz + (above(szz) - szz) + fz)
                planes.append([syy, x, z])
            else:
                y = vy + scale * ((sxy - down(sxy)) - syy + (syz - below(syz)) + fy)
                planes.append([sxy, syz, y])
        return planes

    def completed(turn):
        dens = [received(0, side, 3) for side in range(4)]
        far_syy, far_sxx = corner_in[turn, 0, 0:1], corner_in[turn, 0, 1:2]
        far_syz, far_sxz, far_sxy = corner_in[turn, 1, 0:1], corner_in[turn, 2, 0:1], corner_in[turn, 3, 0:1]
        high_x = (
            received(turn, 0, 1) + dens[0] * (on_row(far_syy, cy - 1, cy) - edge(state.at[6], 1)),
            received(turn, 0, 2) - dens[0] * (on_row(far_syz, 0, cy) + edge(state.at[7], 1)),
        )
        low_x = (received(turn, 1, 2) + dens[1] * (edge(state.at[3], 0) - on_row(far_sxy, 0, cy)),)
        high_y = (
            received(turn, 2, 1) + dens[2] * (on_row(far_sxx, cx - 1, cx) - edge(state.at[6], 3)),
            received(turn, 2, 2) - dens[2] * (on_row(far_sxz, 0, cx) + edge(state.at[8], 3)),
        )
        low_y = (received(turn, 3, 2) + dens[3] * (edge(state.at[4], 2) - on_row(far_sxy, 0, cx)),)
        return high_x, low_x, high_y, low_y

    def forward(step, f):
        return fwd_v[step, f].astype(jnp.float32).reshape(area, cz)

    loads[3].wait()
    loads[4].wait()
    start = [planes + [DT * edge(dens_v, side)] for side, planes in enumerate(advanced(0, False))]
    send_faces(0, start)
    send_corners(0)
    for d in range(1, n_sy):
        rows_copy(0, d).start()
    for side in (0, 1):
        @pl.when(goes[side])
        def _(side=side):
            for d in range(n_sy):
                rows_copy(1 + side, d).start()
    for load in loads[5:]:
        load.wait()

    def force(k, sources, first, stride, count):
        code = (first + stride * lax.broadcasted_iota(jnp.int32, (count, owned), 0)).astype(jnp.float32)
        found = sum(jnp.where(code == rows[comps:comps + 1, :owned], rows[k:k + 1, :owned], 0.0) for rows in sources)
        return jnp.where(first_z[:count], jnp.sum(found, axis=1, keepdims=True), 0.0)

    for d in range(1, n_sy):
        rows_copy(0, d).wait_recv()
    for side in (0, 1):
        @pl.when(comes[side])
        def _(side=side):
            for d in range(n_sy):
                rows_copy(1 + side, d).wait_recv()
    here = [rows_out] + [rows_in.at[0, d] for d in range(1, n_sy)]
    higher, lower = [[rows_in.at[line, d] for d in range(n_sy)] for line in (1, 2)]
    base = iy * area
    for c in range(3):
        forces[c] = force(c, here, base, 1, area)
    beside_force = (
        [force(c, higher, base, 1, cy) for c in (1, 2)],
        [force(0, lower, base + area - cy, 1, cy)],
        [force(c, here, base + area, cy, cx) for c in (0, 2)],
        [force(1, here, base - area + cy - 1, cy, cx)],
    )

    for step in range(steps):
        last = step == steps - 1
        receive_faces(step, [4 if step == 0 else 3] * 4)
        receive_corners(step)
        turn = step
        beside = completed(step)
        if step == 0:
            beside = [
                [v + received(0, side, 3) * f for v, f in zip(beside[side], beside_force[side])] for side in range(4)
            ]
        sxx, syy, szz, sxy, sxz, syz = [state[3 + c] for c in range(6)]
        low_sxy, low_sxz = received(turn, 1, 0), received(turn, 1, 1)
        near_sxy, near_syz = received(turn, 3, 0), received(turn, 3, 1)
        accel_x = (next_x(sxx, received(turn, 0, 0)) - sxx) + (sxy - prev_y(sxy, near_sxy)) + (sxz - below(sxz))
        accel_y = (sxy - prev_x(sxy, low_sxy)) + (next_y(syy, received(turn, 2, 0)) - syy) + (syz - below(syz))
        accel_z = (sxz - prev_x(sxz, low_sxz)) + (syz - prev_y(syz, near_syz)) + (above(szz) - szz)
        scale = DT * dens_v[...]
        change = [scale * (a + forces[3 * step + c]) for c, a in enumerate((accel_x, accel_y, accel_z))]
        for c in range(3):
            state[c] = state[c] + change[c]
        if step == 0:
            for k in range(3, comps):
                forces[k] = force(k, here, base, 1, area)

        rho = sum(forward(step, c) * change[c] for c in range(3))
        total[0] = rho if step == 0 else total[0] + rho
        if last:
            for d in range(1, n_ev):
                kern_copy(d, 0, 1, 0).start()
        strain = [forward(step, 3 + c) for c in range(6)]

        high_x, low_x, high_y, low_y = beside
        vx, vy, vz = [state[c] for c in range(3)]
        exx = vx - prev_x(vx, low_x[0])
        eyy = vy - prev_y(vy, low_y[0])
        ezz = vz - below(vz)
        exy = 0.5 * ((next_y(vx, high_y[0]) - vx) + (next_x(vy, high_x[0]) - vy))
        exz = 0.5 * ((above(vx) - vx) + (next_x(vz, high_x[1]) - vz))
        eyz = 0.5 * ((above(vy) - vy) + (next_y(vz, high_y[1]) - vz))
        rates = (exx, eyy, ezz, exy, exz, eyz)
        trace = exx + eyy + ezz

        def update_stress():
            mu = (DT * 2.0) * shear_v[...]
            common = DT * lame_v[...] * trace
            for c in range(6):
                moved = mu * rates[c]
                state[3 + c] = state[3 + c] + (moved + common if c < 3 else moved)

        def update_kernels():
            lam = DT * (strain[0] + strain[1] + strain[2]) * trace
            total[1] = lam if step == 0 else total[1] + lam
            if last:
                for d in range(1, n_ev):
                    kern_copy(d, 1, 1, 1).start()
            diagonal = strain[0] * exx + strain[1] * eyy + strain[2] * ezz
            others = strain[3] * exy + strain[4] * exz + strain[5] * eyz
            she = (DT * 2.0) * (diagonal + 2.0 * others)
            total[2] = she if step == 0 else total[2] + she

        if last:
            update_kernels()
            for d in range(1, n_ev):
                kern_copy(d, 2, 1, 2).start()
            update_stress()
        else:
            update_stress()
            send_faces(step + 1, advanced(step + 1))
            send_corners(step + 1)
            update_kernels()

    for turn in range(steps):
        for side in range(4):
            @pl.when(goes[side])
            def _(turn=turn, side=side):
                face_copy(turn, side, 4 if turn == 0 else 3).wait_send()
        for g in range(4):
            @pl.when(corner_goes[g])
            def _(turn=turn, g=g):
                corner_copy(turn, g).wait_send()
    for d in range(1, n_sy):
        rows_copy(0, d).wait_send()
    for side in (0, 1):
        @pl.when(goes[side])
        def _(side=side):
            for d in range(n_sy):
                rows_copy(1 + side, d).wait_send()
    for c in range(3):
        for d in range(1, n_ev):
            kern_copy(d, c, 1, c).wait()
        value = total[c]
        for d in range(1, n_ev):
            value = value + kern_in[d - 1, c]
        total[c] = value


def on_device(
    sizes,
    adjoint_state,
    forward_state,
    inv_density,
    lame_lambda,
    shear_modulus,
    station_block,
    station_cell,
    station_trace,
    source_count,
):
    n_sx, n_sy, n_ev = sizes
    fields, cx, cy, cz = adjoint_state.shape[1:]
    steps = forward_state.shape[1]
    owned = station_cell.shape[1]
    area, wide = cx * cy, max(cx, cy)
    hbm = pl.BlockSpec(memory_space=pltpu.HBM)
    lines = -(-(3 * steps + 1) // 8) * 8
    f32, i32 = jnp.float32, jnp.int32
    state, kernels = pl.pallas_call(
        functools.partial(kernel, n_sx, n_sy, n_ev, cx, cy, cz, steps, owned),
        out_shape=(
            jax.ShapeDtypeStruct((fields, area, cz), f32),
            jax.ShapeDtypeStruct((3, area, cz), f32),
        ),
        in_specs=[hbm] * 8 + [pl.BlockSpec(memory_space=pltpu.SMEM)],
        out_specs=[pl.BlockSpec(memory_space=pltpu.VMEM)] * 2,
        scratch_shapes=[
            pltpu.VMEM((3 * steps, area, cz), f32),
            pltpu.VMEM((steps, fields, cx, cy, cz), jnp.bfloat16),
            pltpu.VMEM((area, cz), f32),
            pltpu.VMEM((area, cz), f32),
            pltpu.VMEM((area, cz), f32),
            pltpu.VMEM((1, 1, owned), i32),
            pltpu.VMEM((1, owned), i32),
            pltpu.VMEM((3 * steps, 1, owned), f32),
            pltpu.VMEM((steps, 4, 4, wide, cz), f32),
            pltpu.VMEM((steps, 4, 4, wide, cz), f32),
            pltpu.VMEM((steps, 4, 8, cz), f32),
            pltpu.VMEM((steps, 4, 8, cz), f32),
            pltpu.VMEM((lines, 128), f32),
            pltpu.VMEM((3, n_sy, lines, 128), f32),
            pltpu.VMEM((max(1, n_ev - 1), 3, area, cz), f32),
            pltpu.SemaphoreType.DMA((8,)),
            pltpu.SemaphoreType.DMA((steps, 4)),
            pltpu.SemaphoreType.DMA((steps, 4)),
            pltpu.SemaphoreType.DMA((steps, 4)),
            pltpu.SemaphoreType.DMA((steps, 4)),
            pltpu.SemaphoreType.DMA((3, n_sy)),
            pltpu.SemaphoreType.DMA((3, n_sy)),
            pltpu.SemaphoreType.DMA((max(1, n_ev - 1), 3)),
            pltpu.SemaphoreType.DMA((max(1, n_ev - 1), 3)),
        ],
        compiler_params=pltpu.CompilerParams(
            collective_id=0, has_side_effects=True, vmem_limit_bytes=24 * 1024 * 1024
        ),
    )(
        *(
            pltpu.with_memory_space_constraint(x, pltpu.HBM)
            for x in (
                adjoint_state.reshape(fields, area, cz),
                forward_state[0],
                inv_density.reshape(area, cz),
                lame_lambda.reshape(area, cz),
                shear_modulus.reshape(area, cz),
                station_block.transpose(0, 2, 1),
                station_cell,
                station_trace.transpose(2, 0, 1),
            )
        ),
        source_count,
    )
    return state.reshape(1, fields, cx, cy, cz), kernels.reshape(3, cx, cy, cz)


def solution(mesh):
    sizes = tuple(mesh.shape[name] for name in ("sx", "sy", "ev"))
    return jax.shard_map(
        functools.partial(on_device, sizes),
        mesh=mesh,
        in_specs=(
            P("ev", None, "sx", "sy", None),
            P("ev", None, None, "sx", "sy", None),
            P("sx", "sy", None),
            P("sx", "sy", None),
            P("sx", "sy", None),
            P("ev", ("sx", "sy"), None),
            P("ev", ("sx", "sy")),
            P("ev", ("sx", "sy"), None),
            P("ev", ("sx", "sy")),
        ),
        out_specs=(P("ev", None, "sx", "sy", None), P(None, "sx", "sy", None)),
        check_vma=False,
    )
```
